512 devices in a mesh: pair: 4 (over y_lo, core), slab: 128 (over x, z, y_hi).
Axes of the slice: x: 4, y: 4 (y_hi: 2, y_lo: 2; y = y_hi * 2 + y_lo), z: 16, core: 2. Of those that a mesh axis runs over, the one named last changes fastest.
Arguments:
- amplitudes: bfloat16 [512, 802816], P('pair', 'slab'), may hold values from -24 to 24
- integrals: bfloat16 [256, 802816], P('pair', 'slab'), may hold values from -0.0068359375 to 0.0068359375
- pair_list: int32 [512, 2], P('slab'), may hold values from 0 to 199, as said below
Outputs:
- residual: bfloat16 [512, 256], P('slab', 'pair')
The draws below stay inside these ranges and needn't reach their ends.
Inputs may be any that keep to these rules, and one draw needn't show every extreme that they name: `pair_list`: each row is a packed pair (i, j) with i <= j; no pair appears twice; the pairs (0, 0) and (199, 199) are always present.
All inputs are finite; a program needn't handle non-finite values.
Results may differ from the reference program's by a relative error of at most 0.0051.
Values may be sent and summed in bfloat16 or wider, within the bound.
A program may use at most 128 MiB of HBM per device.

```python
import jax
import jax.numpy as jnp
from jax import lax

NOCC = 200
PAIRS = 512
NVIR = 896
CD = 802816
AB = 256


def draw_pair_list(key, part):
    key = jax.random.fold_in(key, 5)
    first, second = jax.random.split(key)
    packed_total = NOCC * (NOCC + 1) // 2
    inner = jax.random.permutation(first, packed_total - 2)[:PAIRS - 2] + 1
    chosen = jnp.concatenate([inner, jnp.array([0, packed_total - 1], jnp.int32)]).astype(jnp.int32)
    chosen = chosen[jax.random.permutation(second, PAIRS)]
    levels = jnp.arange(NOCC, dtype=jnp.int32)
    starts = levels * (levels + 1) // 2
    upper = jnp.sum((starts[None, :] <= chosen[:, None]).astype(jnp.int32), axis=1) - 1
    lower = chosen - upper * (upper + 1) // 2
    return jnp.stack([lower, upper], axis=1).astype(jnp.int32)


def raised(values, rng, source, target, blocks, factor):
    owner, partner = [(jnp.arange(values.shape[dim]) // (values.shape[dim] // blocks)).reshape([-1 if axis == dim else 1 for axis in range(values.ndim)]) for dim in (source, target)]
    chosen = jax.random.permutation(rng, blocks)[partner]
    strong = (owner == chosen) | (owner == (partner + blocks // 2) % blocks)
    return jnp.where(strong, factor * values, values)


def block_levels(key, dims, pieces, least, largest):
    def one(axis_at, shards_of):
        draws = jax.random.uniform(jax.random.fold_in(jax.random.fold_in(key, 6), axis_at), (shards_of,), jnp.float32, least / len(pieces), largest / len(pieces))
        return jnp.repeat(jnp.exp(draws), dims[axis_at] // shards_of).reshape((-1,) + (1,) * (len(dims) - axis_at - 1))

    loudness = one(*pieces[0])
    for cut in pieces[1:]:
        loudness = loudness * one(*cut)
    return loudness


def bell_draw(rng, dims, width, reach, cuts=(), held_as=jnp.bfloat16):
    result = jax.random.normal(rng, dims, jnp.float32) * width
    if len(cuts) > 0:
        result = block_levels(rng, dims, cuts, -0.22, 0.18) * result
    return jnp.clip(result, min=-reach, max=reach).astype(held_as)


def noise_with(stream_key, shape, scale, bound, cuts, heavy, kind=jnp.bfloat16):
    entries = scale * jax.random.normal(stream_key, shape, jnp.float32)
    if cuts:
        entries = entries * block_levels(stream_key, shape, cuts, -0.22, 0.18)
    return jnp.clip(raised(entries, jax.random.fold_in(stream_key, 3), *heavy), -bound, bound).astype(kind)


def setup_inputs(seed: int = 0) -> dict:
    seeds = jax.random.split(jax.random.key(seed), 4)
    amplitudes = noise_with(seeds[0], (PAIRS, CD), 1.0, 24.0, ((0, 4), (1, 128)), (1, 0, 128, 5.5))
    integrals = bell_draw(seeds[1], (AB, CD), CD ** -0.5, 0.0068359375, ((0, 4), (1, 128)))
    pair_list = draw_pair_list(jax.random.fold_in(seeds[3], 71), 0)
    return {"amplitudes": amplitudes, "integrals": integrals, "pair_list": pair_list}


def reference(amplitudes, integrals, pair_list):
    block = 64
    tiles = amplitudes.reshape(PAIRS // block, block, CD)

    def one_block(tile):
        cube = tile.reshape(block, NVIR, NVIR)
        mirrored = jnp.swapaxes(cube, 1, 2)
        symmetric = (cube.astype(jnp.float32) + mirrored.astype(jnp.float32)).astype(jnp.bfloat16)
        return lax.dot_general(symmetric.reshape(block, CD), integrals, (((1,), (1,)), ((), ())), preferred_element_type=jnp.float32)

    ladder = lax.map(one_block, tiles).reshape(PAIRS, AB)
    weight = jnp.where(pair_list[:, 0] == pair_list[:, 1], 0.5, 1.0).astype(jnp.float32)
    return (ladder * weight[:, None]).astype(jnp.bfloat16)
```

```python
import jax
import jax.numpy as jnp
from jax import lax
from jax.sharding import PartitionSpec as P

C_DEV = 7


def body(amplitudes, integrals, pair_list):
    groups = lax.axis_size("slab")
    rows, width = integrals.shape
    arrived = lax.all_to_all(
        integrals.reshape(rows, C_DEV, groups, C_DEV), "slab", split_axis=2, concat_axis=2, tiled=True
    )
    mirrored = jnp.swapaxes(arrived, 1, 3).reshape(rows, width)
    symmetric = (integrals.astype(jnp.float32) + mirrored.astype(jnp.float32)).astype(jnp.bfloat16)
    whole = lax.all_gather(symmetric, "pair", axis=0, tiled=True)
    part = lax.dot_general(
        amplitudes, whole, (((1,), (1,)), ((), ())), preferred_element_type=jnp.float32
    )
    part = lax.all_to_all(part, "pair", split_axis=1, concat_axis=0, tiled=True)
    terms = lax.all_to_all(
        part.reshape(groups, -1, part.shape[1]), "slab", split_axis=0, concat_axis=0, tiled=True
    )
    ladder = jnp.sum(terms, axis=0)
    weight = jnp.where(pair_list[:, 0] == pair_list[:, 1], 0.5, 1.0).astype(jnp.float32)
    return (ladder * weight[:, None]).astype(jnp.bfloat16)


def solution(mesh):
    placed = (P("pair", "slab"), P("pair", "slab"), P("slab", None))
    return jax.shard_map(
        body, mesh=mesh, in_specs=placed, out_specs=P("slab", "pair"), check_vma=False
    )
```

```python
import jax
import jax.numpy as jnp
from jax import lax
from jax.experimental import pallas as pl
from jax.experimental.pallas import tpu as pltpu
from jax.sharding import PartitionSpec as P

MESH = pl.DeviceIdType.MESH
NV = 896
C = 7
BF = jnp.bfloat16
F32 = jnp.float32


def dot(a, b):
    return jnp.dot(a, b, preferred_element_type=F32)


def dot_nt(a, b):
    return lax.dot_general(a, b, (((1,), (1,)), ((), ())), preferred_element_type=F32)


def iotas(rows, cols):
    return (
        lax.broadcasted_iota(jnp.int32, (rows, cols), 0),
        lax.broadcasted_iota(jnp.int32, (rows, cols), 1),
    )


def one_hot(hit):
    return jnp.where(hit, 1.0, 0.0).astype(BF)


def kernel(
    amp, ints, out,
    i_all, a_all, pick, pack, turn, spread, w, xin, zout, zin, sym, other, aq, acc, r1in, r1sum, r2in,
    load, swap_s, swap_r, xy_s, xy_r, z_s, z_r, lo_s, lo_r, r1_s, r1_r, r2_s, r2_r,
):
    q, s = lax.axis_index("pair"), lax.axis_index("slab")
    l, k = q // 2, q % 2
    x, z, y = s // 32, (s // 2) % 16, s % 2
    me = x * 2 + y
    parity = (z + k) % 2

    def slab(xx, zz, yy):
        return (xx * 16 + zz) * 2 + yy

    def offset(t):
        half = t + 1 - parity
        return (8 - parity - 2 * (half // 2)) * (1 - 2 * (half % 2))

    def goes_to(t):
        return (z + offset(t) + 16) % 16

    def comes_from(t):
        return (z - offset(t) + 16) % 16

    def z_peer(t):
        return (l * 2 + z % 2, slab(x, goes_to(t), y))

    sibling = (l * 2 + 1 - k, s)
    across = ((1 - l) * 2 + k, s)
    near = [((x + a) % 4, (y + b) % 2) for a in range(4) for b in range(2) if a or b]

    barrier = pltpu.get_barrier_semaphore()

    def greet(device):
        pl.semaphore_signal(barrier, inc=1, device_id=device, device_id_type=MESH)

    greet(sibling)
    greet(across)
    for xx, yy in near:
        greet((q, slab(xx, z, yy)))
    for t in range(7):
        greet(z_peer(t))

    @pl.when(parity == 1)
    def _():
        greet(z_peer(7))

    load_i = pltpu.make_async_copy(ints, i_all.at[k], load.at[0])
    load_a = pltpu.make_async_copy(amp, a_all.at[k], load.at[1])
    load_i.start()
    load_a.start()

    r, c = iotas(512, NV)
    m, delta = (r >> 3) & 7, r & 7
    d = 224 * (m >> 1) + 28 * (r >> 6) + 14 * k + 7 * (m & 1) + delta
    pick[...] = one_hot((c == d) & (delta < 7))
    r, c = iotas(400, 512)
    i, j = (c >> 3) & 7, c & 7
    pack[...] = one_hot((r == (c >> 6) * 49 + i * 7 + j) & (i < 7) & (j < 7))
    r, c = iotas(448, 400)
    i = r & 7
    turn[...] = one_hot((c == ((r >> 3) & 7) * 49 + i * 7 + (r >> 6)) & (i < 7))

    def make_spread(g, carry):
        r, c = iotas(NV, 256)
        m, delta = (c >> 3) & 7, c & 7
        d = 224 * (m >> 1) + 28 * (2 * g + (c >> 7)) + 14 * k + 7 * (m & 1) + delta
        hit = (r == d) & (delta < 7)
        upper = ((c >> 6) & 1) == 1
        spread[0, g] = one_hot(hit & ~upper)
        spread[1, g] = one_hot(hit & upper)
        return carry

    lax.fori_loop(0, 4, make_spread, 0)

    load_i.wait()
    load_a.wait()

    @pl.when(parity == 1)
    def _():
        pl.semaphore_wait(barrier, 17)

    @pl.when(parity == 0)
    def _():
        pl.semaphore_wait(barrier, 16)

    def swap(ref, n):
        return pltpu.make_async_remote_copy(
            src_ref=ref.at[k], dst_ref=ref.at[k], send_sem=swap_s.at[n], recv_sem=swap_r.at[n],
            device_id=sibling, device_id_type=MESH,
        )

    def swap_in(ref, n):
        return pltpu.make_async_remote_copy(
            src_ref=ref.at[1 - k], dst_ref=ref.at[1 - k], send_sem=swap_s.at[n], recv_sem=swap_r.at[n],
            device_id=sibling, device_id_type=MESH,
        )

    swap(i_all, 0).start()
    swap_in(i_all, 0).wait_recv()
    swap(a_all, 1).start()

    def rows_of(c):
        return dot_nt(pick[...], i_all[:, :, c * NV:(c + 1) * NV].reshape(128, NV)).reshape(64, 8, 128)

    for a in range(4):
        low = rows_of(2 * a)
        high = rows_of(2 * a + 1) if a < 3 else jnp.zeros_like(low)
        w[:, 16 * a:16 * a + 16, :] = jnp.stack([low, high], axis=1).reshape(64, 16, 128).astype(BF)

    def xy_copy(t, n):
        xx, yy = near[n]
        return pltpu.make_async_remote_copy(
            src_ref=w.at[(goes_to(t) // 2) * 8 + xx * 2 + yy], dst_ref=xin.at[t, me],
            send_sem=xy_s.at[t, n], recv_sem=xy_r.at[t, me],
            device_id=(q, slab(xx, z, yy)), device_id_type=MESH,
        )

    def xy_arrival(t, n):
        xx, yy = near[n]
        there = xx * 2 + yy
        return pltpu.make_async_remote_copy(
            src_ref=xin.at[t, there], dst_ref=xin.at[t, there],
            send_sem=xy_s.at[t, n], recv_sem=xy_r.at[t, there],
            device_id=(q, slab(xx, z, yy)), device_id_type=MESH,
        )

    def send_xy(t, carry):
        for n in range(7):
            xy_copy(t, n).start()
        return carry

    lax.fori_loop(0, 8, send_xy, 0)

    def z_copy(t):
        return pltpu.make_async_remote_copy(
            src_ref=zout.at[t], dst_ref=zin.at[t], send_sem=z_s.at[t], recv_sem=z_r.at[t],
            device_id=z_peer(t), device_id_type=MESH,
        )

    def relay(t, carry):
        xin[t, me] = w[(goes_to(t) // 2) * 8 + me]
        for n in range(7):
            xy_arrival(t, n).wait_recv()
        packed = dot(pack[...], xin[t].reshape(512, 128)).astype(BF)
        stays = offset(t) == 0

        @pl.when(stays)
        def _():
            zin[t] = packed

        @pl.when(jnp.logical_not(stays))
        def _():
            zout[t] = packed
            z_copy(t).start()

        return carry

    lax.fori_loop(0, 8, relay, 0)

    swap_in(a_all, 1).wait_recv()

    def order_amplitudes(g, carry):
        for a in range(4):
            c = 2 * a
            part = dot(a_all[:, :, c * NV:(c + 1) * NV].reshape(256, NV), spread[0, g])
            if a < 3:
                part += dot(a_all[:, :, (c + 1) * NV:(c + 2) * NV].reshape(256, NV), spread[1, g])
            part = part.astype(BF)
            aq[2 * g, :, 128 * a:128 * a + 128] = part[:, :128]
            aq[2 * g + 1, :, 128 * a:128 * a + 128] = part[:, 128:]
        return carry

    lax.fori_loop(0, 4, order_amplitudes, 0)

    acc[...] = jnp.zeros_like(acc)

    def lo_copy(t):
        return pltpu.make_async_remote_copy(
            src_ref=sym.at[t], dst_ref=other.at[t], send_sem=lo_s.at[t], recv_sem=lo_r.at[t],
            device_id=across, device_id_type=MESH,
        )

    def add_other(t):
        lo_copy(t).wait_recv()
        acc[1] += dot(aq[comes_from(t) // 2, :, :448], other[t])

    def symmetrize(t, carry):
        @pl.when(offset(t) != 0)
        def _():
            z_copy(t).wait_recv()

        zeta = comes_from(t) // 2
        mine = w[pl.ds(zeta * 8, 8)].astype(F32).reshape(8, 8, 8, 128)
        mine = jnp.concatenate([mine[:, c].reshape(64, 128) for c in range(C)], axis=0)
        sym[t] = (dot(turn[...], zin[t]) + mine).astype(BF)
        lo_copy(t).start()
        acc[0] += dot(aq[zeta, :, :448], sym[t])

        @pl.when(t > 0)
        def _():
            add_other(t - 1)

        return carry

    lax.fori_loop(0, 8, symmetrize, 0)
    add_other(7)

    mine16 = k * 8 + me

    def r1_copy(n):
        kk, xx, yy = n // 8, (n // 2) % 4, n % 2
        side = jnp.where(yy == l, 0, 1)
        return pltpu.make_async_remote_copy(
            src_ref=acc.at[side, pl.ds(pl.multiple_of(kk * 128 + xx * 32, 32), 32)], dst_ref=r1in.at[mine16],
            send_sem=r1_s.at[n], recv_sem=r1_r.at[mine16],
            device_id=(l * 2 + kk, slab(xx, z, yy)), device_id_type=MESH,
        )

    def r1_arrival(n):
        kk, xx, yy = n // 8, (n // 2) % 4, n % 2
        return pltpu.make_async_remote_copy(
            src_ref=r1in.at[n], dst_ref=r1in.at[n], send_sem=r1_s.at[n], recv_sem=r1_r.at[n],
            device_id=(l * 2 + kk, slab(xx, z, yy)), device_id_type=MESH,
        )

    def r1_send(n, carry):
        @pl.when(n != mine16)
        def _():
            r1_copy(n).start()

        return carry

    lax.fori_loop(0, 16, r1_send, 0)
    total = acc[jnp.where(y == l, 0, 1), pl.ds(pl.multiple_of(k * 128 + x * 32, 32), 32)]
    r1in[mine16] = total

    def r1_wait(n, carry):
        @pl.when(n != mine16)
        def _():
            r1_arrival(n).wait_recv()

        return carry

    lax.fori_loop(0, 16, r1_wait, 0)
    r1sum[...] = jnp.sum(r1in[...], axis=0).reshape(4, 8, 128)

    def r2_owner(n):
        u, yy, cc = n // 4, (n // 2) % 2, n % 2
        return 2 * y + cc, slab(q, 4 * x + u, yy)

    def r2_send(n, carry):
        u = n // 4
        qq, ss = r2_owner(n)
        here = (qq == q) & (ss == s)

        @pl.when(here)
        def _():
            r2in[z] = r1sum[u]

        @pl.when(jnp.logical_not(here))
        def _():
            pltpu.make_async_remote_copy(
                src_ref=r1sum.at[u], dst_ref=r2in.at[z], send_sem=r2_s.at[n], recv_sem=r2_r.at[z],
                device_id=(qq, ss), device_id_type=MESH,
            ).start()

        return carry

    lax.fori_loop(0, 16, r2_send, 0)

    def r2_wait(n, carry):
        qq, ss = x, slab(z // 4, n, q // 2)

        @pl.when(jnp.logical_not((qq == q) & (ss == s)))
        def _():
            pltpu.make_async_remote_copy(
                src_ref=r2in.at[n], dst_ref=r2in.at[n], send_sem=r2_s.at[n], recv_sem=r2_r.at[n],
                device_id=(qq, ss), device_id_type=MESH,
            ).wait_recv()

        return carry

    lax.fori_loop(0, 16, r2_wait, 0)
    done = jnp.sum(r2in[...], axis=0)
    done = jnp.where(y == 0, done[:4], done[4:])
    out[...] = jnp.where(k == 0, done[:, :64], done[:, 64:])

    swap(i_all, 0).wait_send()
    swap(a_all, 1).wait_send()

    def drain(t, carry):
        for n in range(7):
            xy_copy(t, n).wait_send()

        @pl.when(offset(t) != 0)
        def _():
            z_copy(t).wait_send()

        lo_copy(t).wait_send()
        return carry

    lax.fori_loop(0, 8, drain, 0)

    def drain_sums(n, carry):
        @pl.when(n != mine16)
        def _():
            r1_copy(n).wait_send()

        qq, ss = r2_owner(n)

        @pl.when(jnp.logical_not((qq == q) & (ss == s)))
        def _():
            pltpu.make_async_remote_copy(
                src_ref=r1sum.at[n // 4], dst_ref=r2in.at[z], send_sem=r2_s.at[n], recv_sem=r2_r.at[z],
                device_id=(qq, ss), device_id_type=MESH,
            ).wait_send()

        return carry

    lax.fori_loop(0, 16, drain_sums, 0)


def ladder_sum(amplitudes, integrals):
    dma = pltpu.SemaphoreType.DMA
    return pl.pallas_call(
        kernel,
        out_shape=jax.ShapeDtypeStruct((4, 64), F32),
        in_specs=[pl.BlockSpec(memory_space=pl.ANY)] * 2,
        out_specs=pl.BlockSpec(memory_space=pltpu.VMEM),
        scratch_shapes=[
            pltpu.VMEM((2, 64, C * NV), BF),
            pltpu.VMEM((2, 128, C * NV), BF),
            pltpu.VMEM((512, NV), BF),
            pltpu.VMEM((400, 512), BF),
            pltpu.VMEM((448, 400), BF),
            pltpu.VMEM((2, 4, NV, 256), BF),
            pltpu.VMEM((64, 64, 128), BF),
            pltpu.VMEM((8, 8, 64, 128), BF),
            pltpu.VMEM((8, 400, 128), BF),
            pltpu.VMEM((8, 400, 128), BF),
            pltpu.VMEM((8, 448, 128), BF),
            pltpu.VMEM((8, 448, 128), BF),
            pltpu.VMEM((8, 256, 512), BF),
            pltpu.VMEM((2, 256, 128), F32),
            pltpu.VMEM((16, 32, 128), F32),
            pltpu.VMEM((4, 8, 128), F32),
            pltpu.VMEM((16, 8, 128), F32),
            dma((2,)), dma((2,)), dma((2,)), dma((8, 8)), dma((8, 8)), dma((8,)), dma((8,)), dma((8,)), dma((8,)),
            dma((16,)), dma((16,)), dma((16,)), dma((16,)),
        ],
        compiler_params=pltpu.CompilerParams(
            collective_id=0, has_side_effects=True, vmem_limit_bytes=48 * 1024 * 1024
        ),
        cost_estimate=pl.CostEstimate(flops=4 * 10**9, bytes_accessed=2 * 10**7, transcendentals=0),
        name="ladder_sum",
    )(amplitudes, integrals)


def body(amplitudes, integrals, pair_list):
    ladder = ladder_sum(amplitudes, integrals)
    weight = jnp.where(pair_list[:, 0] == pair_list[:, 1], 0.5, 1.0).astype(jnp.float32)
    return (ladder * weight[:, None]).astype(BF)


def solution(mesh):
    placed = (P("pair", "slab"), P("pair", "slab"), P("slab", None))
    return jax.shard_map(
        body, mesh=mesh, in_specs=placed, out_specs=P("slab", "pair"), check_vma=False
    )
```

```python
import jax
import jax.numpy as jnp
from jax import lax
from jax.experimental import pallas as pl
from jax.experimental.pallas import tpu as pltpu
from jax.sharding import PartitionSpec as P

MESH = pl.DeviceIdType.MESH
NV = 896
C = 7
BF = jnp.bfloat16
F32 = jnp.float32
SEND = (3, 2, 4, 1, 5, 0, 6, 7)
TAKE = (3, 2, 1, 4, 0, 5, 6, 7)


def entry(table, t):
    value = jnp.int32(table[0])
    for n in range(1, len(table)):
        value = jnp.where(t == n, table[n], value)
    return value


def dot(a, b):
    return jnp.dot(a, b, preferred_element_type=F32)


def dot_nt(a, b):
    return lax.dot_general(a, b, (((1,), (1,)), ((), ())), preferred_element_type=F32)


def iotas(rows, cols):
    return (
        lax.broadcasted_iota(jnp.int32, (rows, cols), 0),
        lax.broadcasted_iota(jnp.int32, (rows, cols), 1),
    )


def one_hot(hit):
    return jnp.where(hit, 1.0, 0.0).astype(BF)


def kernel(
    amp, ints, pairs, out,
    i_all, a_all, pick, pack, turn, spread, w, xin, zout, zin, sym, other, aq, acc, r1in, r1sum, r2in, ij,
    load, swap_s, swap_r, xy_s, xy_r, z_s, z_r, lo_s, lo_r, r1_s, r1_r, r2_s, r2_r,
):
    q, s = lax.axis_index("pair"), lax.axis_index("slab")
    l, k = q // 2, q % 2
    x, z, y = s // 32, (s // 2) % 16, s % 2
    me = x * 2 + y
    parity = (z + k) % 2

    def slab(xx, zz, yy):
        return (xx * 16 + zz) * 2 + yy

    def offset(t):
        half = 8 - t - parity
        return (8 - parity - 2 * (half // 2)) * (1 - 2 * (half % 2))

    def goes_to(t):
        return (z + offset(t) + 16) % 16

    def comes_from(t):
        return (z - offset(t) + 16) % 16

    def z_peer(t):
        return (l * 2 + z % 2, slab(x, goes_to(t), y))

    sibling = (l * 2 + 1 - k, s)
    across = ((1 - l) * 2 + k, s)
    steps = [(a, b) for a in range(4) for b in range(2) if a or b]
    near = [((x + a) % 4, (y + b) % 2) for a, b in steps]
    back = [steps.index(((4 - a) % 4, b)) for a, b in steps]

    barrier = pltpu.get_barrier_semaphore()

    def greet(device):
        pl.semaphore_signal(barrier, inc=1, device_id=device, device_id_type=MESH)

    greet(sibling)
    greet(across)
    for xx, yy in near:
        greet((q, slab(xx, z, yy)))
    for t in range(1, 8):
        greet(z_peer(t))

    @pl.when(parity == 1)
    def _():
        greet(z_peer(0))

    load_i = pltpu.make_async_copy(ints, i_all.at[k], load.at[0])
    load_a = pltpu.make_async_copy(amp, a_all.at[k], load.at[1])
    load_i.start()
    load_a.start()
    load_p = pltpu.make_async_copy(pairs, ij, load.at[2])
    load_p.start()

    r, c = iotas(512, NV)
    m, delta = (r >> 3) & 7, r & 7
    d = 224 * (m >> 1) + 28 * (r >> 6) + 14 * k + 7 * (m & 1) + delta
    pick[...] = one_hot((c == d) & (delta < 7))

    load_i.wait()

    @pl.when(parity == 1)
    def _():
        pl.semaphore_wait(barrier, 17)

    @pl.when(parity == 0)
    def _():
        pl.semaphore_wait(barrier, 16)

    def swap(ref, n):
        return pltpu.make_async_remote_copy(
            src_ref=ref, dst_ref=ref, send_sem=swap_s.at[n], recv_sem=swap_r.at[n],
            device_id=sibling, device_id_type=MESH,
        )

    def part(core, a):
        return i_all.at[core, :, pl.ds(2 * a * NV, NV if a == 3 else 2 * NV)]

    for a in range(4):
        swap(part(k, a), a).start()

    def rows_of(c):
        return dot_nt(pick[...], i_all[:, :, c * NV:(c + 1) * NV].reshape(128, NV)).reshape(64, 8, 128)

    for a in range(4):
        swap(part(1 - k, a), a).wait_recv()
        low = rows_of(2 * a)
        high = rows_of(2 * a + 1) if a < 3 else jnp.zeros_like(low)
        w[:, 16 * a:16 * a + 16, :] = jnp.stack([low, high], axis=1).reshape(64, 16, 128).astype(BF)

    def xy_copy(t, n):
        xx, yy = near[n]
        return pltpu.make_async_remote_copy(
            src_ref=w.at[(goes_to(t) // 2) * 8 + xx * 2 + yy], dst_ref=xin.at[t, back[n]],
            send_sem=xy_s.at[t, n], recv_sem=xy_r.at[t, back[n]],
            device_id=(q, slab(xx, z, yy)), device_id_type=MESH,
        )

    def xy_arrival(t, n):
        xx, yy = near[n]
        return pltpu.make_async_remote_copy(
            src_ref=xin.at[t, n], dst_ref=xin.at[t, n],
            send_sem=xy_s.at[t, n], recv_sem=xy_r.at[t, n],
            device_id=(q, slab(xx, z, yy)), device_id_type=MESH,
        )

    def send_xy(t, carry):
        t = entry(SEND, t)
        for n in range(7):
            xy_copy(t, n).start()
        return carry


    def own_copy(t):
        return pltpu.make_async_remote_copy(
            src_ref=w.at[(goes_to(t) // 2) * 8 + me], dst_ref=zin.at[t, pl.ds(0, 64)],
            send_sem=z_s.at[0, t], recv_sem=z_r.at[0, t], device_id=z_peer(t), device_id_type=MESH,
        )

    def z_copy(t):
        return pltpu.make_async_remote_copy(
            src_ref=zout.at[t], dst_ref=zin.at[t, pl.ds(64, 352)],
            send_sem=z_s.at[1, t], recv_sem=z_r.at[1, t], device_id=z_peer(t), device_id_type=MESH,
        )

    def send_own(t, carry):
        t = entry(SEND, t)
        stays = offset(t) == 0

        @pl.when(stays)
        def _():
            zin[t, pl.ds(0, 64)] = w[(goes_to(t) // 2) * 8 + me]

        @pl.when(jnp.logical_not(stays))
        def _():
            own_copy(t).start()

        return carry

    lax.fori_loop(0, 8, send_own, 0)
    lax.fori_loop(0, 8, send_xy, 0)
    load_a.wait()
    load_p.wait()
    swap(a_all.at[k], 4).start()

    r, c = iotas(352, 448)
    i, j = (c >> 3) & 7, c & 7
    pack[...] = one_hot((r == (c >> 6) * 49 + i * 7 + j) & (i < 7) & (j < 7))

    def relay(t, carry):
        t = entry(SEND, t)
        for n in range(7):
            xy_arrival(t, n).wait_recv()
        packed = dot(pack[...], xin[t].reshape(448, 128)).astype(BF)
        stays = offset(t) == 0

        @pl.when(stays)
        def _():
            zin[t, pl.ds(64, 352)] = packed

        @pl.when(jnp.logical_not(stays))
        def _():
            zout[t] = packed
            z_copy(t).start()

        return carry

    lax.fori_loop(0, 8, relay, 0)

    def make_spread(g, carry):
        r, c = iotas(NV, 256)
        m, delta = (c >> 3) & 7, c & 7
        d = 224 * (m >> 1) + 28 * (2 * g + (c >> 7)) + 14 * k + 7 * (m & 1) + delta
        hit = (r == d) & (delta < 7)
        upper = ((c >> 6) & 1) == 1
        spread[0, g] = one_hot(hit & ~upper)
        spread[1, g] = one_hot(hit & upper)
        return carry

    lax.fori_loop(0, 4, make_spread, 0)

    r, c = iotas(448, 416)
    i, j, m = r & 7, r >> 6, (r >> 3) & 7
    n = (((m >> 1) - x) & 3) * 2 + (((m & 1) - y) & 1)
    turn[...] = one_hot((c == jnp.where(n == 0, i * 8 + j, 15 + n * 49 + i * 7 + j)) & (i < 7))

    swap(a_all.at[1 - k], 4).wait_recv()

    def order_amplitudes(g, carry):
        for a in range(4):
            c = 2 * a
            part = dot(a_all[:, :, c * NV:(c + 1) * NV].reshape(256, NV), spread[0, g])
            if a < 3:
                part += dot(a_all[:, :, (c + 1) * NV:(c + 2) * NV].reshape(256, NV), spread[1, g])
            part = part.astype(BF)
            aq[2 * g, :, 128 * a:128 * a + 128] = part[:, :128]
            aq[2 * g + 1, :, 128 * a:128 * a + 128] = part[:, 128:]
        return carry

    lax.fori_loop(0, 4, order_amplitudes, 0)

    acc[...] = jnp.zeros_like(acc)

    def lo_copy(t):
        return pltpu.make_async_remote_copy(
            src_ref=sym.at[t], dst_ref=other.at[t], send_sem=lo_s.at[t], recv_sem=lo_r.at[t],
            device_id=across, device_id_type=MESH,
        )

    def add_other(t):
        lo_copy(t).wait_recv()
        acc[1] += dot(aq[comes_from(t) // 2, :, :448], other[t])

    def symmetrize(step, carry):
        t = entry(TAKE, step)

        @pl.when(offset(t) != 0)
        def _():
            own_copy(t).wait_recv()
            z_copy(t).wait_recv()

        zeta = comes_from(t) // 2
        mine = w[pl.ds(zeta * 8, 8)].astype(F32).reshape(8, 8, 8, 128)
        mine = jnp.concatenate([mine[:, c].reshape(64, 128) for c in range(C)], axis=0)
        sym[t] = (dot(turn[...], zin[t]) + mine).astype(BF)
        lo_copy(t).start()
        acc[0] += dot(aq[zeta, :, :448], sym[t])

        @pl.when(step > 0)
        def _():
            add_other(entry(TAKE, step - 1))

        return carry

    lax.fori_loop(0, 8, symmetrize, 0)
    add_other(TAKE[7])

    mine16 = k * 8 + me

    def r1_copy(n):
        kk, xx, yy = n // 8, (n // 2) % 4, n % 2
        side = jnp.where(yy == l, 0, 1)
        return pltpu.make_async_remote_copy(
            src_ref=acc.at[side, pl.ds(pl.multiple_of(kk * 128 + xx * 32, 32), 32)], dst_ref=r1in.at[mine16],
            send_sem=r1_s.at[n], recv_sem=r1_r.at[mine16],
            device_id=(l * 2 + kk, slab(xx, z, yy)), device_id_type=MESH,
        )

    def r1_arrival(n):
        kk, xx, yy = n // 8, (n // 2) % 4, n % 2
        return pltpu.make_async_remote_copy(
            src_ref=r1in.at[n], dst_ref=r1in.at[n], send_sem=r1_s.at[n], recv_sem=r1_r.at[n],
            device_id=(l * 2 + kk, slab(xx, z, yy)), device_id_type=MESH,
        )

    def r1_send(n, carry):
        @pl.when(n != mine16)
        def _():
            r1_copy(n).start()

        return carry

    lax.fori_loop(0, 16, r1_send, 0)
    total = acc[jnp.where(y == l, 0, 1), pl.ds(pl.multiple_of(k * 128 + x * 32, 32), 32)]
    r1in[mine16] = total

    for a in range(4):
        swap(part(k, a), a).wait_send()
    swap(a_all.at[k], 4).wait_send()

    def drain(t, carry):
        for n in range(7):
            xy_copy(t, n).wait_send()

        @pl.when(offset(t) != 0)
        def _():
            own_copy(t).wait_send()
            z_copy(t).wait_send()

        lo_copy(t).wait_send()
        return carry

    lax.fori_loop(0, 8, drain, 0)

    def r1_wait(n, carry):
        @pl.when(n != mine16)
        def _():
            r1_arrival(n).wait_recv()

        return carry

    lax.fori_loop(0, 16, r1_wait, 0)
    r1sum[...] = jnp.sum(r1in[...], axis=0).reshape(4, 8, 128)

    def r2_owner(n):
        u, yy, cc = n // 4, (n // 2) % 2, n % 2
        return 2 * y + cc, slab(q, 4 * x + u, yy)

    def r2_copy(n):
        qq, ss = r2_owner(n)
        return pltpu.make_async_remote_copy(
            src_ref=r1sum.at[n // 4], dst_ref=r2in.at[z], send_sem=r2_s.at[n], recv_sem=r2_r.at[z],
            device_id=(qq, ss), device_id_type=MESH,
        )

    def r2_send(n, carry):
        u = n // 4
        qq, ss = r2_owner(n)
        here = (qq == q) & (ss == s)

        @pl.when(here)
        def _():
            r2in[z] = r1sum[u]

        @pl.when(jnp.logical_not(here))
        def _():
            r2_copy(n).start()

        return carry

    lax.fori_loop(0, 16, r2_send, 0)

    def drain_sums(n, carry):
        @pl.when(n != mine16)
        def _():
            r1_copy(n).wait_send()

        return carry

    lax.fori_loop(0, 16, drain_sums, 0)

    def r2_wait(n, carry):
        qq, ss = x, slab(z // 4, n, q // 2)

        @pl.when(jnp.logical_not((qq == q) & (ss == s)))
        def _():
            pltpu.make_async_remote_copy(
                src_ref=r2in.at[n], dst_ref=r2in.at[n], send_sem=r2_s.at[n], recv_sem=r2_r.at[n],
                device_id=(qq, ss), device_id_type=MESH,
            ).wait_recv()

        return carry

    lax.fori_loop(0, 16, r2_wait, 0)
    done = jnp.sum(r2in[...], axis=0)
    done = jnp.where(y == 0, done[:4], done[4:])
    done = jnp.where(k == 0, done[:, :64], done[:, 64:])
    weight = jnp.where(ij[0:1] == ij[1:2], 0.5, 1.0)
    r, c = iotas(4, 4)
    weight = jnp.sum(jnp.where(r == c, weight, 0.0), axis=1, keepdims=True)
    out[...] = done * weight

    def drain_tiles(n, carry):
        qq, ss = r2_owner(n)

        @pl.when(jnp.logical_not((qq == q) & (ss == s)))
        def _():
            r2_copy(n).wait_send()

        return carry

    lax.fori_loop(0, 16, drain_tiles, 0)


def ladder_sum(amplitudes, integrals, pair_list):
    dma = pltpu.SemaphoreType.DMA
    return pl.pallas_call(
        kernel,
        out_shape=jax.ShapeDtypeStruct((4, 64), F32),
        in_specs=[pl.BlockSpec(memory_space=pltpu.HBM)] * 3,
        out_specs=pl.BlockSpec(memory_space=pltpu.VMEM),
        scratch_shapes=[
            pltpu.VMEM((2, 64, C * NV), BF),
            pltpu.VMEM((2, 128, C * NV), BF),
            pltpu.VMEM((512, NV), BF),
            pltpu.VMEM((352, 448), BF),
            pltpu.VMEM((448, 416), BF),
            pltpu.VMEM((2, 4, NV, 256), BF),
            pltpu.VMEM((64, 64, 128), BF),
            pltpu.VMEM((8, 7, 64, 128), BF),
            pltpu.VMEM((8, 352, 128), BF),
            pltpu.VMEM((8, 416, 128), BF),
            pltpu.VMEM((8, 448, 128), BF),
            pltpu.VMEM((8, 448, 128), BF),
            pltpu.VMEM((8, 256, 512), BF),
            pltpu.VMEM((2, 256, 128), F32),
            pltpu.VMEM((16, 32, 128), F32),
            pltpu.VMEM((4, 8, 128), F32),
            pltpu.VMEM((16, 8, 128), F32),
            pltpu.VMEM((2, 4), jnp.int32),
            dma((3,)), dma((5,)), dma((5,)), dma((8, 7)), dma((8, 7)), dma((2, 8)), dma((2, 8)), dma((8,)), dma((8,)),
            dma((16,)), dma((16,)), dma((16,)), dma((16,)),
        ],
        compiler_params=pltpu.CompilerParams(
            collective_id=0, has_side_effects=True, vmem_limit_bytes=127 * 512 * 1024
        ),
        cost_estimate=pl.CostEstimate(flops=4 * 10**9, bytes_accessed=2 * 10**7, transcendentals=0),
        name="ladder_sum",
    )(amplitudes, integrals, pair_list.T)


def body(amplitudes, integrals, pair_list):
    return ladder_sum(amplitudes, integrals, pair_list).astype(BF)


def solution(mesh):
    placed = (P("pair", "slab"), P("pair", "slab"), P("slab", None))
    return jax.shard_map(
        body, mesh=mesh, in_specs=placed, out_specs=P("slab", "pair"), check_vma=False
    )
```

```python
import jax
import jax.numpy as jnp
from jax import lax
from jax.experimental import pallas as pl
from jax.experimental.pallas import tpu as pltpu
from jax.sharding import PartitionSpec as P

MESH = pl.DeviceIdType.MESH
NV = 896
C = 7
BF = jnp.bfloat16
F32 = jnp.float32
SEND = (3, 2, 4, 1, 5, 0, 6, 7)
TAKE = (3, 2, 1, 4, 0, 5, 6, 7)


def entry(table, t):
    value = jnp.int32(table[0])
    for n in range(1, len(table)):
        value = jnp.where(t == n, table[n], value)
    return value


def dot(a, b):
    return jnp.dot(a, b, preferred_element_type=F32)


def dot_nt(a, b):
    return lax.dot_general(a, b, (((1,), (1,)), ((), ())), preferred_element_type=F32)


def iotas(rows, cols):
    return (
        lax.broadcasted_iota(jnp.int32, (rows, cols), 0),
        lax.broadcasted_iota(jnp.int32, (rows, cols), 1),
    )


def one_hot(hit):
    return jnp.where(hit, 1.0, 0.0).astype(BF)


def kernel(
    amp, ints, pairs, out,
    i_all, a_all, pick, pack, turn, spread, w, xin, zout, zin, sym, other, aq, acc, r1in, r1sum, r2in, ij,
    load, swap_s, swap_r, xy_s, xy_r, z_s, z_r, lo_s, lo_r, r1_s, r1_r, r2_s, r2_r,
):
    q, s = lax.axis_index("pair"), lax.axis_index("slab")
    l, k = q // 2, q % 2
    x, z, y = s // 32, (s // 2) % 16, s % 2
    me = x * 2 + y
    parity = (z + k) % 2

    def slab(xx, zz, yy):
        return (xx * 16 + zz) * 2 + yy

    def offset(t):
        half = 8 - t - parity
        return (8 - parity - 2 * (half // 2)) * (1 - 2 * (half % 2))

    def goes_to(t):
        return (z + offset(t) + 16) % 16

    def comes_from(t):
        return (z - offset(t) + 16) % 16

    def z_peer(t):
        return (l * 2 + z % 2, slab(x, goes_to(t), y))

    sibling = (l * 2 + 1 - k, s)
    across = ((1 - l) * 2 + k, s)
    steps = [(a, b) for a in range(4) for b in range(2) if a or b]
    near = [((x + a) % 4, (y + b) % 2) for a, b in steps]
    back = [steps.index(((4 - a) % 4, b)) for a, b in steps]

    barrier = pltpu.get_barrier_semaphore()

    def greet(device):
        pl.semaphore_signal(barrier, inc=1, device_id=device, device_id_type=MESH)

    greet(sibling)
    greet(across)
    for xx, yy in near:
        greet((q, slab(xx, z, yy)))
    for t in range(1, 8):
        greet(z_peer(t))

    @pl.when(parity == 1)
    def _():
        greet(z_peer(0))

    load_i = pltpu.make_async_copy(ints, i_all.at[k], load.at[0])
    load_a = pltpu.make_async_copy(amp, a_all.at[k], load.at[1])
    load_i.start()
    load_a.start()
    load_p = pltpu.make_async_copy(pairs, ij, load.at[2])
    load_p.start()

    r, c = iotas(512, NV)
    m, delta = (r >> 3) & 7, r & 7
    d = 224 * (m >> 1) + 28 * (r >> 6) + 14 * k + 7 * (m & 1) + delta
    pick[...] = one_hot((c == d) & (delta < 7))

    load_i.wait()

    @pl.when(parity == 1)
    def _():
        pl.semaphore_wait(barrier, 17)

    @pl.when(parity == 0)
    def _():
        pl.semaphore_wait(barrier, 16)

    def swap(ref, n):
        return pltpu.make_async_remote_copy(
            src_ref=ref, dst_ref=ref, send_sem=swap_s.at[n], recv_sem=swap_r.at[n],
            device_id=sibling, device_id_type=MESH,
        )

    def part(core, a):
        return i_all.at[core, :, pl.ds(2 * a * NV, NV if a == 3 else 2 * NV)]

    for a in range(4):
        swap(part(k, a), a).start()

    def rows_of(c):
        return dot_nt(pick[...], i_all[:, :, c * NV:(c + 1) * NV].reshape(128, NV)).reshape(64, 8, 128)

    for a in range(4):
        swap(part(1 - k, a), a).wait_recv()
        low = rows_of(2 * a)
        high = rows_of(2 * a + 1) if a < 3 else jnp.zeros_like(low)
        w[:, 16 * a:16 * a + 16, :] = jnp.stack([low, high], axis=1).reshape(64, 16, 128).astype(BF)

    def xy_copy(t, n):
        xx, yy = near[n]
        return pltpu.make_async_remote_copy(
            src_ref=w.at[(goes_to(t) // 2) * 8 + xx * 2 + yy], dst_ref=xin.at[t, back[n]],
            send_sem=xy_s.at[0], recv_sem=xy_r.at[t],
            device_id=(q, slab(xx, z, yy)), device_id_type=MESH,
        )

    def arrived(ref, sem):
        pltpu.make_async_copy(ref, ref, sem).wait()

    def send_xy(t, carry):
        t = entry(SEND, t)
        for n in range(7):
            xy_copy(t, n).start()
        return carry


    def own_copy(t):
        return pltpu.make_async_remote_copy(
            src_ref=w.at[(goes_to(t) // 2) * 8 + me], dst_ref=zin.at[t, pl.ds(0, 64)],
            send_sem=z_s.at[0], recv_sem=z_r.at[0, t], device_id=z_peer(t), device_id_type=MESH,
        )

    def z_copy(t):
        return pltpu.make_async_remote_copy(
            src_ref=zout.at[t], dst_ref=zin.at[t, pl.ds(64, 352)],
            send_sem=z_s.at[1], recv_sem=z_r.at[1, t], device_id=z_peer(t), device_id_type=MESH,
        )

    def send_own(t, carry):
        t = entry(SEND, t)
        stays = offset(t) == 0

        @pl.when(stays)
        def _():
            zin[t, pl.ds(0, 64)] = w[(goes_to(t) // 2) * 8 + me]

        @pl.when(jnp.logical_not(stays))
        def _():
            own_copy(t).start()

        return carry

    lax.fori_loop(0, 8, send_own, 0)
    lax.fori_loop(0, 8, send_xy, 0)
    load_a.wait()
    load_p.wait()
    swap(a_all.at[k], 4).start()

    r, c = iotas(352, 448)
    i, j = (c >> 3) & 7, c & 7
    pack[...] = one_hot((r == (c >> 6) * 49 + i * 7 + j) & (i < 7) & (j < 7))

    def relay(t, carry):
        t = entry(SEND, t)
        arrived(xin.at[t], xy_r.at[t])
        packed = dot(pack[...], xin[t].reshape(448, 128)).astype(BF)
        stays = offset(t) == 0

        @pl.when(stays)
        def _():
            zin[t, pl.ds(64, 352)] = packed

        @pl.when(jnp.logical_not(stays))
        def _():
            zout[t] = packed
            z_copy(t).start()

        return carry

    lax.fori_loop(0, 8, relay, 0)

    def make_spread(g, carry):
        r, c = iotas(NV, 256)
        m, delta = (c >> 3) & 7, c & 7
        d = 224 * (m >> 1) + 28 * (2 * g + (c >> 7)) + 14 * k + 7 * (m & 1) + delta
        hit = (r == d) & (delta < 7)
        upper = ((c >> 6) & 1) == 1
        spread[0, g] = one_hot(hit & ~upper)
        spread[1, g] = one_hot(hit & upper)
        return carry

    lax.fori_loop(0, 4, make_spread, 0)

    r, c = iotas(448, 416)
    i, j, m = r & 7, r >> 6, (r >> 3) & 7
    n = (((m >> 1) - x) & 3) * 2 + (((m & 1) - y) & 1)
    turn[...] = one_hot((c == jnp.where(n == 0, i * 8 + j, 15 + n * 49 + i * 7 + j)) & (i < 7))

    swap(a_all.at[1 - k], 4).wait_recv()

    def order_amplitudes(g, carry):
        for a in range(4):
            c = 2 * a
            part = dot(a_all[:, :, c * NV:(c + 1) * NV].reshape(256, NV), spread[0, g])
            if a < 3:
                part += dot(a_all[:, :, (c + 1) * NV:(c + 2) * NV].reshape(256, NV), spread[1, g])
            part = part.astype(BF)
            aq[2 * g, :, 128 * a:128 * a + 128] = part[:, :128]
            aq[2 * g + 1, :, 128 * a:128 * a + 128] = part[:, 128:]
        return carry

    lax.fori_loop(0, 4, order_amplitudes, 0)

    acc[...] = jnp.zeros_like(acc)

    def lo_copy(t):
        return pltpu.make_async_remote_copy(
            src_ref=sym.at[t], dst_ref=other.at[t], send_sem=lo_s.at[0], recv_sem=lo_r.at[t],
            device_id=across, device_id_type=MESH,
        )

    def add_other(t):
        lo_copy(t).wait_recv()
        acc[1] += dot(aq[comes_from(t) // 2, :, :448], other[t])

    def symmetrize(step, carry):
        t = entry(TAKE, step)

        @pl.when(offset(t) != 0)
        def _():
            own_copy(t).wait_recv()
            z_copy(t).wait_recv()

        zeta = comes_from(t) // 2
        mine = w[pl.ds(zeta * 8, 8)].astype(F32).reshape(8, 8, 8, 128)
        mine = jnp.concatenate([mine[:, c].reshape(64, 128) for c in range(C)], axis=0)
        sym[t] = (dot(turn[...], zin[t]) + mine).astype(BF)
        lo_copy(t).start()
        acc[0] += dot(aq[zeta, :, :448], sym[t])

        @pl.when(step > 0)
        def _():
            add_other(entry(TAKE, step - 1))

        return carry

    lax.fori_loop(0, 8, symmetrize, 0)

    mine16 = k * 8 + me

    def r1_copy(n):
        kk, xx, yy = n // 8, (n // 2) % 4, n % 2
        side = jnp.where(yy == l, 0, 1)
        return pltpu.make_async_remote_copy(
            src_ref=acc.at[side, pl.ds(pl.multiple_of(kk * 128 + xx * 32, 32), 32)], dst_ref=r1in.at[mine16],
            send_sem=r1_s.at[0], recv_sem=r1_r.at[0],
            device_id=(l * 2 + kk, slab(xx, z, yy)), device_id_type=MESH,
        )

    def r1_send(n, carry):
        @pl.when(n != mine16)
        def _():
            r1_copy(n).start()

        return carry

    lax.fori_loop(0, 8, lambda i, carry: r1_send(2 * i + l, carry), 0)
    add_other(TAKE[7])
    lax.fori_loop(0, 8, lambda i, carry: r1_send(2 * i + 1 - l, carry), 0)
    total = acc[jnp.where(y == l, 0, 1), pl.ds(pl.multiple_of(k * 128 + x * 32, 32), 32)]
    r1in[mine16] = total

    for a in range(4):
        swap(part(k, a), a).wait_send()
    swap(a_all.at[k], 4).wait_send()
    arrived(w.at[pl.ds(0, 56)], xy_s.at[0])
    arrived(sym, lo_s.at[0])

    @pl.when(parity == 1)
    def _():
        arrived(w.at[pl.ds(0, 8)], z_s.at[0])
        arrived(zout, z_s.at[1])

    @pl.when(parity == 0)
    def _():
        arrived(w.at[pl.ds(0, 7)], z_s.at[0])
        arrived(zout.at[pl.ds(0, 7)], z_s.at[1])

    arrived(r1in.at[pl.ds(0, 15)], r1_r.at[0])
    r1sum[...] = jnp.sum(r1in[...], axis=0).reshape(4, 8, 128)

    def r2_owner(n):
        u, yy, cc = n // 4, (n // 2) % 2, n % 2
        return 2 * y + cc, slab(q, 4 * x + u, yy)

    def r2_copy(n):
        qq, ss = r2_owner(n)
        return pltpu.make_async_remote_copy(
            src_ref=r1sum.at[n // 4], dst_ref=r2in.at[z], send_sem=r2_s.at[0], recv_sem=r2_r.at[0],
            device_id=(qq, ss), device_id_type=MESH,
        )

    def r2_send(n, carry):
        u = n // 4
        qq, ss = r2_owner(n)
        here = (qq == q) & (ss == s)

        @pl.when(here)
        def _():
            r2in[z] = r1sum[u]

        @pl.when(jnp.logical_not(here))
        def _():
            r2_copy(n).start()

        return carry

    lax.fori_loop(0, 16, r2_send, 0)

    arrived(r1in.at[pl.ds(0, 15)], r1_s.at[0])

    takes_own = (x == q) & (z // 4 == x) & (q // 2 == y)

    def tiles(sem):
        @pl.when(takes_own)
        def _():
            arrived(r2in.at[pl.ds(0, 15)], sem)

        @pl.when(jnp.logical_not(takes_own))
        def _():
            arrived(r2in, sem)

    tiles(r2_r.at[0])

    done = jnp.sum(r2in[...], axis=0)
    done = jnp.where(y == 0, done[:4], done[4:])
    done = jnp.where(k == 0, done[:, :64], done[:, 64:])
    weight = jnp.where(ij[0:1] == ij[1:2], 0.5, 1.0)
    r, c = iotas(4, 4)
    weight = jnp.sum(jnp.where(r == c, weight, 0.0), axis=1, keepdims=True)
    out[...] = done * weight

    tiles(r2_s.at[0])


def ladder_sum(amplitudes, integrals, pair_list):
    dma = pltpu.SemaphoreType.DMA
    return pl.pallas_call(
        kernel,
        out_shape=jax.ShapeDtypeStruct((4, 64), F32),
        in_specs=[pl.BlockSpec(memory_space=pltpu.HBM)] * 3,
        out_specs=pl.BlockSpec(memory_space=pltpu.VMEM),
        scratch_shapes=[
            pltpu.VMEM((2, 64, C * NV), BF),
            pltpu.VMEM((2, 128, C * NV), BF),
            pltpu.VMEM((512, NV), BF),
            pltpu.VMEM((352, 448), BF),
            pltpu.VMEM((448, 416), BF),
            pltpu.VMEM((2, 4, NV, 256), BF),
            pltpu.VMEM((64, 64, 128), BF),
            pltpu.VMEM((8, 7, 64, 128), BF),
            pltpu.VMEM((8, 352, 128), BF),
            pltpu.VMEM((8, 416, 128), BF),
            pltpu.VMEM((8, 448, 128), BF),
            pltpu.VMEM((8, 448, 128), BF),
            pltpu.VMEM((8, 256, 512), BF),
            pltpu.VMEM((2, 256, 128), F32),
            pltpu.VMEM((16, 32, 128), F32),
            pltpu.VMEM((4, 8, 128), F32),
            pltpu.VMEM((16, 8, 128), F32),
            pltpu.VMEM((2, 4), jnp.int32),
            dma((3,)), dma((5,)), dma((5,)), dma((1,)), dma((8,)), dma((2,)), dma((2, 8)), dma((1,)), dma((8,)),
            dma((1,)), dma((1,)), dma((1,)), dma((1,)),
        ],
        compiler_params=pltpu.CompilerParams(
            collective_id=0, has_side_effects=True, vmem_limit_bytes=127 * 512 * 1024
        ),
        cost_estimate=pl.CostEstimate(flops=4 * 10**9, bytes_accessed=2 * 10**7, transcendentals=0),
        name="ladder_sum",
    )(amplitudes, integrals, pair_list.T)


def body(amplitudes, integrals, pair_list):
    return ladder_sum(amplitudes, integrals, pair_list).astype(BF)


def solution(mesh):
    placed = (P("pair", "slab"), P("pair", "slab"), P("slab", None))
    return jax.shard_map(
        body, mesh=mesh, in_specs=placed, out_specs=P("slab", "pair"), check_vma=False
    )
```

```python
import jax
import jax.numpy as jnp
from jax import lax
from jax.experimental import pallas as pl
from jax.experimental.pallas import tpu as pltpu
from jax.sharding import PartitionSpec as P

MESH = pl.DeviceIdType.MESH
NV = 896
C = 7
BF = jnp.bfloat16
F32 = jnp.float32
SEND = (3, 2, 4, 1, 5, 0, 6, 7)
TAKE = (3, 2, 1, 4, 0, 5, 6, 7)


def entry(table, t):
    value = jnp.int32(table[0])
    for n in range(1, len(table)):
        value = jnp.where(t == n, table[n], value)
    return value


def dot(a, b):
    return jnp.dot(a, b, preferred_element_type=F32)


def dot_nt(a, b):
    return lax.dot_general(a, b, (((1,), (1,)), ((), ())), preferred_element_type=F32)


def iotas(rows, cols):
    return (
        lax.broadcasted_iota(jnp.int32, (rows, cols), 0),
        lax.broadcasted_iota(jnp.int32, (rows, cols), 1),
    )


def one_hot(hit):
    return jnp.where(hit, 1.0, 0.0).astype(BF)


def kernel(
    amp, ints, pairs, out,
    i_all, a_all, pick, pack, turn, spread, w, xin, zout, zin, sym, other, aq, acc, r1in, r1sum, r2in, ij,
    load, swap_s, swap_r, xy_s, xy_r, z_s, z_r, lo_s, lo_r, r1_s, r1_r, r2_s, r2_r,
):
    q, s = lax.axis_index("pair"), lax.axis_index("slab")
    l, k = q // 2, q % 2
    x, z, y = s // 32, (s // 2) % 16, s % 2
    me = x * 2 + y
    parity = (z + k) % 2

    def slab(xx, zz, yy):
        return (xx * 16 + zz) * 2 + yy

    def offset(t):
        half = 8 - t - parity
        return (8 - parity - 2 * (half // 2)) * (1 - 2 * (half % 2))

    def goes_to(t):
        return (z + offset(t) + 16) % 16

    def comes_from(t):
        return (z - offset(t) + 16) % 16

    def z_peer(t):
        return (l * 2 + z % 2, slab(x, goes_to(t), y))

    sibling = (l * 2 + 1 - k, s)
    across = ((1 - l) * 2 + k, s)
    steps = [(a, b) for a in range(4) for b in range(2) if a or b]
    near = [((x + a) % 4, (y + b) % 2) for a, b in steps]
    back = [steps.index(((4 - a) % 4, b)) for a, b in steps]

    barrier = pltpu.get_barrier_semaphore()

    def greet(device):
        pl.semaphore_signal(barrier, inc=1, device_id=device, device_id_type=MESH)

    greet(sibling)
    greet(across)
    for xx, yy in near:
        greet((q, slab(xx, z, yy)))
    for t in range(1, 8):
        greet(z_peer(t))

    @pl.when(parity == 1)
    def _():
        greet(z_peer(0))

    load_i = pltpu.make_async_copy(ints, i_all.at[k], load.at[0])
    load_a = pltpu.make_async_copy(amp, a_all.at[k], load.at[1])
    load_i.start()
    load_a.start()
    load_p = pltpu.make_async_copy(pairs, ij, load.at[2])
    load_p.start()

    r, c = iotas(512, NV)
    m, delta = (r >> 3) & 7, r & 7
    d = 224 * (m >> 1) + 28 * (r >> 6) + 14 * k + 7 * (m & 1) + delta
    pick[...] = one_hot((c == d) & (delta < 7))

    load_i.wait()

    @pl.when(parity == 1)
    def _():
        pl.semaphore_wait(barrier, 17)

    @pl.when(parity == 0)
    def _():
        pl.semaphore_wait(barrier, 16)

    def swap(ref, n):
        return pltpu.make_async_remote_copy(
            src_ref=ref, dst_ref=ref, send_sem=swap_s.at[n], recv_sem=swap_r.at[n],
            device_id=sibling, device_id_type=MESH,
        )

    def part(core, a):
        return i_all.at[core, :, pl.ds(2 * a * NV, NV if a == 3 else 2 * NV)]

    for a in range(4):
        swap(part(k, a), a).start()

    def rows_of(c):
        return dot_nt(pick[...], i_all[:, :, c * NV:(c + 1) * NV].reshape(128, NV)).reshape(64, 8, 128)

    for a in range(4):
        swap(part(1 - k, a), a).wait_recv()
        low = rows_of(2 * a)
        high = rows_of(2 * a + 1) if a < 3 else jnp.zeros_like(low)
        w[:, 16 * a:16 * a + 16, :] = jnp.stack([low, high], axis=1).reshape(64, 16, 128).astype(BF)

    def xy_copy(t, n):
        xx, yy = near[n]
        return pltpu.make_async_remote_copy(
            src_ref=w.at[(goes_to(t) // 2) * 8 + xx * 2 + yy], dst_ref=xin.at[t, back[n]],
            send_sem=xy_s.at[0], recv_sem=xy_r.at[t],
            device_id=(q, slab(xx, z, yy)), device_id_type=MESH,
        )

    def arrived(ref, sem):
        pltpu.make_async_copy(ref, ref, sem).wait()

    def send_xy(t, carry):
        t = entry(SEND, t)
        for n in range(7):
            xy_copy(t, n).start()
        return carry


    def own_copy(t):
        return pltpu.make_async_remote_copy(
            src_ref=w.at[(goes_to(t) // 2) * 8 + me], dst_ref=zin.at[t, pl.ds(0, 64)],
            send_sem=z_s.at[0], recv_sem=z_r.at[0, t], device_id=z_peer(t), device_id_type=MESH,
        )

    def z_copy(t):
        return pltpu.make_async_remote_copy(
            src_ref=zout.at[t], dst_ref=zin.at[t, pl.ds(64, 352)],
            send_sem=z_s.at[1], recv_sem=z_r.at[1, t], device_id=z_peer(t), device_id_type=MESH,
        )

    def z_half(t, h):
        return pltpu.make_async_remote_copy(
            src_ref=zout.at[t, pl.ds(176 * h, 176)], dst_ref=zin.at[t, pl.ds(64 + 176 * h, 176)],
            send_sem=z_s.at[1], recv_sem=z_r.at[1, t], device_id=z_peer(t), device_id_type=MESH,
        )

    def send_own(t, carry):
        t = entry(SEND, t)
        stays = offset(t) == 0

        @pl.when(stays)
        def _():
            zin[t, pl.ds(0, 64)] = w[(goes_to(t) // 2) * 8 + me]

        @pl.when(jnp.logical_not(stays))
        def _():
            own_copy(t).start()

        return carry

    lax.fori_loop(0, 8, send_own, 0)
    lax.fori_loop(0, 8, send_xy, 0)
    load_a.wait()
    load_p.wait()
    swap(a_all.at[k], 4).start()

    r, c = iotas(352, 448)
    i, j = (c >> 3) & 7, c & 7
    pack[...] = one_hot((r == (c >> 6) * 49 + i * 7 + j) & (i < 7) & (j < 7))

    def relay(t, carry):
        t = entry(SEND, t)
        arrived(xin.at[t], xy_r.at[t])
        packed = dot(pack[...], xin[t].reshape(448, 128)).astype(BF)
        stays = offset(t) == 0

        @pl.when(stays)
        def _():
            zin[t, pl.ds(64, 352)] = packed

        @pl.when(jnp.logical_not(stays))
        def _():
            zout[t] = packed
            for h in range(2):
                z_half(t, h).start()

        return carry

    lax.fori_loop(0, 8, relay, 0)

    def make_spread(g, carry):
        r, c = iotas(NV, 256)
        m, delta = (c >> 3) & 7, c & 7
        d = 224 * (m >> 1) + 28 * (2 * g + (c >> 7)) + 14 * k + 7 * (m & 1) + delta
        hit = (r == d) & (delta < 7)
        upper = ((c >> 6) & 1) == 1
        spread[0, g] = one_hot(hit & ~upper)
        spread[1, g] = one_hot(hit & upper)
        return carry

    lax.fori_loop(0, 4, make_spread, 0)

    r, c = iotas(448, 416)
    i, j, m = r & 7, r >> 6, (r >> 3) & 7
    n = (((m >> 1) - x) & 3) * 2 + (((m & 1) - y) & 1)
    turn[...] = one_hot((c == jnp.where(n == 0, i * 8 + j, 15 + n * 49 + i * 7 + j)) & (i < 7))

    swap(a_all.at[1 - k], 4).wait_recv()

    def order_amplitudes(g, carry):
        for a in range(4):
            c = 2 * a
            part = dot(a_all[:, :, c * NV:(c + 1) * NV].reshape(256, NV), spread[0, g])
            if a < 3:
                part += dot(a_all[:, :, (c + 1) * NV:(c + 2) * NV].reshape(256, NV), spread[1, g])
            part = part.astype(BF)
            aq[2 * g, :, 128 * a:128 * a + 128] = part[:, :128]
            aq[2 * g + 1, :, 128 * a:128 * a + 128] = part[:, 128:]
        return carry

    lax.fori_loop(0, 4, order_amplitudes, 0)

    acc[...] = jnp.zeros_like(acc)

    def lo_copy(t):
        return pltpu.make_async_remote_copy(
            src_ref=sym.at[t], dst_ref=other.at[t], send_sem=lo_s.at[0], recv_sem=lo_r.at[t],
            device_id=across, device_id_type=MESH,
        )

    def add_other(t):
        lo_copy(t).wait_recv()
        acc[1] += dot(aq[comes_from(t) // 2, :, :448], other[t])

    def symmetrize(step, carry):
        t = entry(TAKE, step)

        @pl.when(offset(t) != 0)
        def _():
            own_copy(t).wait_recv()
            z_copy(t).wait_recv()

        zeta = comes_from(t) // 2
        mine = w[pl.ds(zeta * 8, 8)].astype(F32).reshape(8, 8, 8, 128)
        mine = jnp.concatenate([mine[:, c].reshape(64, 128) for c in range(C)], axis=0)
        sym[t] = (dot(turn[...], zin[t]) + mine).astype(BF)
        lo_copy(t).start()
        acc[0] += dot(aq[zeta, :, :448], sym[t])

        @pl.when(step > 0)
        def _():
            add_other(entry(TAKE, step - 1))

        return carry

    lax.fori_loop(0, 8, symmetrize, 0)

    mine16 = k * 8 + me

    def r1_copy(n):
        kk, xx, yy = n // 8, (n // 2) % 4, n % 2
        side = jnp.where(yy == l, 0, 1)
        return pltpu.make_async_remote_copy(
            src_ref=acc.at[side, pl.ds(pl.multiple_of(kk * 128 + xx * 32, 32), 32)], dst_ref=r1in.at[mine16],
            send_sem=r1_s.at[0], recv_sem=r1_r.at[0],
            device_id=(l * 2 + kk, slab(xx, z, yy)), device_id_type=MESH,
        )

    def r1_send(n, carry):
        @pl.when(n != mine16)
        def _():
            r1_copy(n).start()

        return carry

    lax.fori_loop(0, 8, lambda i, carry: r1_send(2 * i + l, carry), 0)
    add_other(TAKE[7])
    lax.fori_loop(0, 8, lambda i, carry: r1_send(2 * i + 1 - l, carry), 0)
    total = acc[jnp.where(y == l, 0, 1), pl.ds(pl.multiple_of(k * 128 + x * 32, 32), 32)]
    r1in[mine16] = total

    for a in range(4):
        swap(part(k, a), a).wait_send()
    swap(a_all.at[k], 4).wait_send()
    arrived(w.at[pl.ds(0, 56)], xy_s.at[0])
    arrived(sym, lo_s.at[0])

    @pl.when(parity == 1)
    def _():
        arrived(w.at[pl.ds(0, 8)], z_s.at[0])
        arrived(zout, z_s.at[1])

    @pl.when(parity == 0)
    def _():
        arrived(w.at[pl.ds(0, 7)], z_s.at[0])
        arrived(zout.at[pl.ds(0, 7)], z_s.at[1])

    arrived(r1in.at[pl.ds(0, 15)], r1_r.at[0])
    r1sum[...] = jnp.sum(r1in[...], axis=0).reshape(4, 8, 128)

    def r2_owner(n):
        u, yy, cc = n // 4, (n // 2) % 2, n % 2
        return 2 * y + cc, slab(q, 4 * x + u, yy)

    def r2_copy(n):
        qq, ss = r2_owner(n)
        return pltpu.make_async_remote_copy(
            src_ref=r1sum.at[n // 4], dst_ref=r2in.at[z], send_sem=r2_s.at[0], recv_sem=r2_r.at[0],
            device_id=(qq, ss), device_id_type=MESH,
        )

    def r2_send(n, carry):
        u = n // 4
        qq, ss = r2_owner(n)
        here = (qq == q) & (ss == s)

        @pl.when(here)
        def _():
            r2in[z] = r1sum[u]

        @pl.when(jnp.logical_not(here))
        def _():
            r2_copy(n).start()

        return carry

    lax.fori_loop(0, 16, r2_send, 0)

    arrived(r1in.at[pl.ds(0, 15)], r1_s.at[0])

    takes_own = (x == q) & (z // 4 == x) & (q // 2 == y)

    def tiles(sem):
        @pl.when(takes_own)
        def _():
            arrived(r2in.at[pl.ds(0, 15)], sem)

        @pl.when(jnp.logical_not(takes_own))
        def _():
            arrived(r2in, sem)

    tiles(r2_r.at[0])

    done = jnp.sum(r2in[...], axis=0)
    done = jnp.where(y == 0, done[:4], done[4:])
    done = jnp.where(k == 0, done[:, :64], done[:, 64:])
    weight = jnp.where(ij[0:1] == ij[1:2], 0.5, 1.0)
    r, c = iotas(4, 4)
    weight = jnp.sum(jnp.where(r == c, weight, 0.0), axis=1, keepdims=True)
    out[...] = done * weight

    tiles(r2_s.at[0])


def ladder_sum(amplitudes, integrals, pair_list):
    dma = pltpu.SemaphoreType.DMA
    return pl.pallas_call(
        kernel,
        out_shape=jax.ShapeDtypeStruct((4, 64), F32),
        in_specs=[pl.BlockSpec(memory_space=pltpu.HBM)] * 3,
        out_specs=pl.BlockSpec(memory_space=pltpu.VMEM),
        scratch_shapes=[
            pltpu.VMEM((2, 64, C * NV), BF),
            pltpu.VMEM((2, 128, C * NV), BF),
            pltpu.VMEM((512, NV), BF),
            pltpu.VMEM((352, 448), BF),
            pltpu.VMEM((448, 416), BF),
            pltpu.VMEM((2, 4, NV, 256), BF),
            pltpu.VMEM((64, 64, 128), BF),
            pltpu.VMEM((8, 7, 64, 128), BF),
            pltpu.VMEM((8, 352, 128), BF),
            pltpu.VMEM((8, 416, 128), BF),
            pltpu.VMEM((8, 448, 128), BF),
            pltpu.VMEM((8, 448, 128), BF),
            pltpu.VMEM((8, 256, 512), BF),
            pltpu.VMEM((2, 256, 128), F32),
            pltpu.VMEM((16, 32, 128), F32),
            pltpu.VMEM((4, 8, 128), F32),
            pltpu.VMEM((16, 8, 128), F32),
            pltpu.VMEM((2, 4), jnp.int32),
            dma((3,)), dma((5,)), dma((5,)), dma((1,)), dma((8,)), dma((2,)), dma((2, 8)), dma((1,)), dma((8,)),
            dma((1,)), dma((1,)), dma((1,)), dma((1,)),
        ],
        compiler_params=pltpu.CompilerParams(
            collective_id=0, has_side_effects=True, vmem_limit_bytes=127 * 512 * 1024
        ),
        cost_estimate=pl.CostEstimate(flops=4 * 10**9, bytes_accessed=2 * 10**7, transcendentals=0),
        name="ladder_sum",
    )(amplitudes, integrals, pair_list.T)


def body(amplitudes, integrals, pair_list):
    return ladder_sum(amplitudes, integrals, pair_list).astype(BF)


def solution(mesh):
    placed = (P("pair", "slab"), P("pair", "slab"), P("slab", None))
    return jax.shard_map(
        body, mesh=mesh, in_specs=placed, out_specs=P("slab", "pair"), check_vma=False
    )
```
